32 devices in a mesh: seq: 8 (over z, x), ch: 4 (over y, core).
Axes of the slice: x: 2, y: 2, z: 4, core: 2. Of those that a mesh axis runs over, the one named last changes fastest.
Arguments:
- queries_in: bfloat16 [2048, 8192], P('seq', 'ch'), may hold values from -160 to 160
- keys_in: bfloat16 [2048, 8192], P('seq', 'ch'), may hold values from -8 to 8
- values_in: bfloat16 [2048, 8192], P('seq', 'ch'), may hold values from -6 to 6
- gate_branch: bfloat16 [2048, 8192], P('seq', 'ch'), may hold values from -6 to 6
- key_branch: bfloat16 [2048, 8192], P('seq', 'ch'), may hold values from -6 to 6
- mr_filter: bfloat16 [128, 8192], P(None, 'ch'), may hold values from -3 to 3
- out_grad: bfloat16 [2048, 8192], P('seq', 'ch'), may hold values from -40 to 40
- doc_ids: int32 [2048], replicated, may hold values from 0 to 15, never falling along the last dimension, each value on 1 to 1024 neighbouring positions
Outputs:
- query_grad: bfloat16 [2048, 8192], P('seq', 'ch')
- key_grad: bfloat16 [2048, 8192], P('seq', 'ch')
- value_grad: bfloat16 [2048, 8192], P('seq', 'ch')
- gate_grad: bfloat16 [2048, 8192], P('seq', 'ch')
- branch_grad: bfloat16 [2048, 8192], P('seq', 'ch')
- filter_step: float32 [128, 8192], P('seq', 'ch')
The draws below stay inside these ranges and needn't reach their ends.
Inputs may be any that keep to these rules, and one draw needn't show every extreme that they name: `doc_ids`: document numbers never fall along the sequence; each document has 1 to 1024 tokens and one has exactly 1024.
All inputs are finite; a program needn't handle non-finite values.
Results may differ from the reference program's by a relative error of at most 0.009.
Values may be sent and summed in bfloat16 or wider, within the bound.
A program may use at most 128 MiB of HBM per device.

```python
import math
import jax
import jax.numpy as jnp
import numpy as np
from jax import lax

D = 8192
HD = 128
TAPS = 128
TOK_DEV = 256
SPAN = 4
HEADS = 64
TOKENS = 2048
MOST = 1024
DOCS = 16
N_SEQ = 8


def attention_pair(key):
    base = jax.random.fold_in(key, 11)
    query_key, key_key = jax.random.split(base, 2)
    key_rows = jax.random.normal(key_key, (TOKENS, D), jnp.float32)
    query_rows = jax.random.normal(query_key, (TOKENS, D), jnp.float32)
    return (query_rows, key_rows)


def draw_queries_in(key, part):
    return attention_pair(key)[0].astype(jnp.bfloat16)


def draw_keys_in(key, part):
    return attention_pair(key)[1].astype(jnp.bfloat16)


def draw_out_grad(key, part):
    first, second = jax.random.split(jax.random.fold_in(key, 23))
    channel = jnp.arange(D, dtype=jnp.float32) / (D - 1)
    spread = jnp.exp(jax.random.uniform(second, (D,), jnp.float32, 0.0, math.log(10.0))) / 3.0
    values = jnp.clip(jax.random.normal(first, (TOKENS, D), jnp.float32), -6.0, 6.0)
    rising = jnp.exp(math.log(3.0) * channel) / 1.7
    return (values * spread[None, :] * rising[None, :]).astype(jnp.bfloat16)


def draw_mr_filter(key, part):
    first = jax.random.fold_in(key, 37)
    channel = jnp.arange(D, dtype=jnp.float32) / (D - 1)
    values = 0.15 * jnp.clip(jax.random.normal(first, (TAPS, D), jnp.float32), -6.0, 6.0)
    rising = jnp.exp(math.log(3.0) * channel)
    return (values * rising[None, :]).astype(jnp.bfloat16)


def steps_of(stream_key, dims, shards, least, high):
    loudness = 1.0
    for axis_at, blocks in shards:
        steps = jax.random.uniform(jax.random.fold_in(jax.random.fold_in(stream_key, 6), axis_at), (blocks,), jnp.float32, least / len(shards), high / len(shards))
        loudness = loudness * jnp.repeat(jnp.exp(steps), dims[axis_at] // blocks).reshape((-1,) + (1,) * (len(dims) - 1 - axis_at))
    return loudness


def profile(amount, total, bound, lean):
    loads = [(1 << 20) // math.isqrt(rank ** lean) + 1 for rank in range(2, amount + 1)]
    spare, counts = total - bound - (amount - 1), [1] * (amount - 1)
    while spare > 0:
        movable = [i for i in range(amount - 1) if counts[i] < bound]
        mass, remaining = sum([loads[i] for i in movable]), spare
        for i in movable:
            more = min(bound - counts[i], max(1, remaining * loads[i] // mass), spare)
            counts[i] = counts[i] + more
            spare = spare - more
    return np.array([bound] + counts)


def ragged_sizes(stream_key, count, total, most, slope):
    if count == 2:
        one = jax.random.randint(stream_key, (), max(1, total - most), min(most, total - 1) + 1)
        return jnp.stack([one, total - one])
    tallies = jnp.asarray(profile(count, total, most, slope), jnp.int32)
    pairs = (count - 1) // 2
    donor, receiver = tallies[1:1 + 2 * pairs:2], tallies[2:2 + 2 * pairs:2]
    room = jnp.minimum(donor - 1, most - receiver)
    shifted = jax.random.randint(jax.random.fold_in(stream_key, 1), (pairs,), 0, 1 << 20) % (room + 1)
    tallies = tallies.at[1:1 + 2 * pairs:2].set(donor - shifted).at[2:2 + 2 * pairs:2].set(receiver + shifted)
    return tallies[jax.random.permutation(jax.random.fold_in(stream_key, 2), count)]


def noise(own_key, extent, deviation, bound, pieces=(), kind=jnp.bfloat16):
    loudness = steps_of(own_key, extent, pieces, -0.22, 0.18) if pieces else 1.0
    values = jax.random.normal(own_key, extent, jnp.float32) * deviation * loudness
    return jnp.minimum(jnp.maximum(values, -bound), bound).astype(kind)


def setup_inputs(seed: int = 0) -> dict:
    streams_of = jax.random.split(jax.random.key(seed), 9)
    queries_in = draw_queries_in(jax.random.fold_in(streams_of[8], 71), 0)
    keys_in = draw_keys_in(jax.random.fold_in(streams_of[8], 71), 0)
    values_in = noise(streams_of[2], (TOKENS, D), 1.0, 6.0, ((0, 8), (1, 4)))
    gate_branch = noise(streams_of[3], (TOKENS, D), 1.0, 6.0, ((0, 8), (1, 4)))
    key_branch = noise(streams_of[4], (TOKENS, D), 1.0, 6.0, ((0, 8), (1, 4)))
    mr_filter = draw_mr_filter(jax.random.fold_in(streams_of[8], 71), 0)
    out_grad = draw_out_grad(jax.random.fold_in(streams_of[8], 71), 0)
    doc_ids = jnp.searchsorted(jnp.cumsum(ragged_sizes(streams_of[7], DOCS, TOKENS, MOST, 2)), jnp.arange(TOKENS), side="right").astype(jnp.int32)
    return dict(queries_in=queries_in, keys_in=keys_in, values_in=values_in, gate_branch=gate_branch, key_branch=key_branch, mr_filter=mr_filter, out_grad=out_grad, doc_ids=doc_ids)


def causal_conv(extended, weights_in):
    rows = extended.shape[0] - (TAPS - 1)

    def add_tap(tap, total):
        index = jnp.asarray(tap).astype(jnp.int32)
        piece = lax.dynamic_slice_in_dim(extended, (TAPS - 1 - index).astype(jnp.int32), rows, 0).astype(jnp.float32)
        weight_row = lax.dynamic_index_in_dim(weights_in, index, 0, keepdims=False).astype(jnp.float32)
        return total + weight_row[None, :] * piece
    return lax.fori_loop(0, TAPS, add_tap, jnp.zeros((rows, extended.shape[1]), jnp.float32))

def anti_conv(extended, weights_in):
    rows = extended.shape[0] - (TAPS - 1)

    def add_tap(tap, total):
        index = jnp.asarray(tap).astype(jnp.int32)
        piece = lax.dynamic_slice_in_dim(extended, index, rows, 0).astype(jnp.float32)
        weight_row = lax.dynamic_index_in_dim(weights_in, index, 0, keepdims=False).astype(jnp.float32)
        return total + weight_row[None, :] * piece
    return lax.fori_loop(0, TAPS, add_tap, jnp.zeros((rows, extended.shape[1]), jnp.float32))

def filter_corr(extended, gradient):
    rows = gradient.shape[0]
    grad_float = gradient.astype(jnp.float32)

    def one_tap(tap):
        piece = lax.dynamic_slice_in_dim(extended, (TAPS - 1 - tap).astype(jnp.int32), rows, 0).astype(jnp.float32)
        return lax.optimization_barrier(jnp.sum(grad_float * piece, 0))
    return lax.map(one_tap, jnp.arange(TAPS, dtype=jnp.int32))

def reference(queries_in, keys_in, values_in, gate_branch, key_branch, mr_filter, out_grad, doc_ids):
    window = (SPAN + 1) * TOK_DEV
    score_scale = HD ** (-0.5)
    front = jnp.zeros((SPAN * TOK_DEV, D), jnp.bfloat16)
    key_pad = jnp.concatenate([front, keys_in], 0)
    value_pad = jnp.concatenate([front, values_in], 0)
    doc_pad = jnp.concatenate([jnp.full((SPAN * TOK_DEV,), -1, jnp.int32), doc_ids], 0)
    blocks = jnp.arange(N_SEQ, dtype=jnp.int32)

    def block_scores(block):
        start = (block * TOK_DEV).astype(jnp.int32)
        query_rows = lax.dynamic_slice_in_dim(queries_in, start, TOK_DEV, 0).astype(jnp.float32).reshape(TOK_DEV, HEADS, HD)
        key_rows = lax.dynamic_slice_in_dim(key_pad, start, window, 0).astype(jnp.float32).reshape(window, HEADS, HD)
        value_rows = lax.dynamic_slice_in_dim(value_pad, start, window, 0).astype(jnp.float32).reshape(window, HEADS, HD)
        query_doc = lax.dynamic_slice_in_dim(doc_ids, start, TOK_DEV, 0)
        key_doc = lax.dynamic_slice_in_dim(doc_pad, start, window, 0)
        query_pos = start + jnp.arange(TOK_DEV, dtype=jnp.int32)
        key_pos = start - SPAN * TOK_DEV + jnp.arange(window, dtype=jnp.int32)
        allowed = (query_doc[:, None] == key_doc[None, :]) & (key_pos[None, :] <= query_pos[:, None])
        scores = jnp.einsum('qhd,khd->hqk', query_rows, key_rows) * score_scale
        scores = jnp.where(allowed[None], scores, -jnp.inf)
        return (scores, allowed, query_rows, key_rows, value_rows)

    def forward(block):
        scores, allowed, query_rows, key_rows, value_rows = block_scores(block)
        row_max = lax.optimization_barrier(jnp.max(scores, -1))
        log_total = row_max + jnp.log(lax.optimization_barrier(jnp.sum(jnp.exp(scores - row_max[..., None]), -1)))
        weights = jnp.where(allowed[None], jnp.exp(scores - log_total[..., None]), 0.0)
        probs = weights.astype(jnp.bfloat16)
        output = jnp.einsum('hqk,khd->qhd', probs.astype(jnp.float32), value_rows)
        return (output.astype(jnp.bfloat16).reshape(TOK_DEV, D), log_total)
    attn_blocks, totals = lax.map(forward, blocks)
    attn_out = attn_blocks.reshape(TOKENS, D)
    mixed = (key_branch.astype(jnp.float32) * attn_out.astype(jnp.float32)).astype(jnp.bfloat16)
    mixed_ext = jnp.concatenate([jnp.zeros((TAPS - 1, D), jnp.bfloat16), mixed], 0)
    conv_out = causal_conv(mixed_ext, mr_filter)
    gate_grad = (out_grad.astype(jnp.float32) * conv_out).astype(jnp.bfloat16)
    conv_grad = (out_grad.astype(jnp.float32) * gate_branch.astype(jnp.float32)).astype(jnp.bfloat16)
    grad_ext = jnp.concatenate([conv_grad, jnp.zeros((TAPS - 1, D), jnp.bfloat16)], 0)
    mixed_grad = anti_conv(grad_ext, mr_filter)
    filter_grad = filter_corr(mixed_ext, conv_grad)
    branch_grad = (mixed_grad * attn_out.astype(jnp.float32)).astype(jnp.bfloat16)
    attn_grad = (mixed_grad * key_branch.astype(jnp.float32)).astype(jnp.bfloat16)

    def backward(carry, inputs):
        key_acc, value_acc = carry
        block, log_total = inputs
        start = (block * TOK_DEV).astype(jnp.int32)
        scores, allowed, query_rows, key_rows, value_rows = block_scores(block)
        weights = jnp.where(allowed[None], jnp.exp(scores - log_total[..., None]), 0.0)
        probs = weights.astype(jnp.bfloat16).astype(jnp.float32)
        grad_rows = lax.dynamic_slice_in_dim(attn_grad, start, TOK_DEV, 0).astype(jnp.float32).reshape(TOK_DEV, HEADS, HD)
        out_rows = lax.dynamic_slice_in_dim(attn_out, start, TOK_DEV, 0).astype(jnp.float32).reshape(TOK_DEV, HEADS, HD)
        row_dot = jnp.einsum('qhd,qhd->hq', grad_rows, out_rows)
        prob_grad = jnp.einsum('qhd,khd->hqk', grad_rows, value_rows)
        score_grad = (weights * (prob_grad - row_dot[..., None])).astype(jnp.bfloat16).astype(jnp.float32)
        query_part = (jnp.einsum('hqk,khd->qhd', score_grad, key_rows) * score_scale).astype(jnp.bfloat16).reshape(TOK_DEV, D)
        key_terms = (jnp.einsum('hqk,qhd->khd', score_grad, query_rows) * score_scale).reshape(window, D)
        value_terms = jnp.einsum('hqk,qhd->khd', probs, grad_rows).reshape(window, D)
        key_acc = lax.dynamic_update_slice_in_dim(key_acc, lax.dynamic_slice_in_dim(key_acc, start, window, 0) + key_terms, start, 0)
        value_acc = lax.dynamic_update_slice_in_dim(value_acc, lax.dynamic_slice_in_dim(value_acc, start, window, 0) + value_terms, start, 0)
        return ((key_acc, value_acc), query_part)
    empty = jnp.zeros(((N_SEQ + SPAN) * TOK_DEV, D), jnp.float32)
    (key_acc, value_acc), query_parts = lax.scan(backward, (empty, empty), (blocks, totals))
    query_grad = query_parts.reshape(TOKENS, D)
    key_grad = key_acc[SPAN * TOK_DEV:].astype(jnp.bfloat16)
    value_grad = value_acc[SPAN * TOK_DEV:].astype(jnp.bfloat16)
    filter_sq = jnp.sum(jnp.square(mr_filter.astype(jnp.float32)))
    trust = jnp.sqrt(filter_sq) / jnp.sqrt(jnp.sum(filter_grad * filter_grad) + 1e-06)
    filter_step = trust * filter_grad
    return (query_grad, key_grad, value_grad, gate_grad, branch_grad, filter_step)
```

```python
import functools
import jax
import jax.numpy as jnp
from jax import lax
from jax.experimental import pallas as pl
from jax.experimental.pallas import tpu as pltpu
from jax.sharding import PartitionSpec as P

HD = 128
TAPS = 128
SPAN = 4
CHUNKS = 2
VMEM = 40 * 1024 * 1024


def from_behind(array, axis, by):
    size = lax.axis_size(axis)
    pairs = [(i, i + by) for i in range(size) if 0 <= i + by < size]
    return lax.ppermute(array, axis, pairs)


def causal_conv(extended, weights_in):
    channels = extended.shape[1]
    kernel = weights_in[:, None, :]
    result = lax.conv_general_dilated(
        extended[None],
        kernel,
        (1,),
        "VALID",
        dimension_numbers=("NWC", "WIO", "NWC"),
        feature_group_count=channels,
        preferred_element_type=jnp.float32,
    )
    return result[0]


def anti_conv(extended, weights_in):
    channels = extended.shape[1]
    kernel = weights_in[:, None, :]
    result = lax.conv_general_dilated(
        extended[None],
        kernel,
        (1,),
        "VALID",
        dimension_numbers=("NWC", "WIO", "NWC"),
        feature_group_count=channels,
        preferred_element_type=jnp.float32,
    )
    return result[0]


def filter_corr(extended, gradient):
    channels = extended.shape[1]
    kernel = gradient[:, None, :]
    result = lax.conv_general_dilated(
        extended[None],
        kernel,
        (1,),
        "VALID",
        dimension_numbers=("NWC", "WIO", "NWC"),
        feature_group_count=channels,
        preferred_element_type=jnp.float32,
    )
    return result[0]


def exchange(array):
    size = lax.axis_size("seq")
    return lax.ppermute(array, "seq", [(i, i ^ 1) for i in range(size)])


def dot(a, b, dims):
    return lax.dot_general(a, b, (dims, ((), ())), preferred_element_type=jnp.float32)


def attention_kernel(*refs):
    bias, queries, key_branch, mixed_grad = refs[:4]
    keys, values = refs[4 : 5 + SPAN], refs[5 + SPAN : 6 + 2 * SPAN]
    mixed_out, branch_out, query_out, own_out = refs[6 + 2 * SPAN : 10 + 2 * SPAN]
    earlier_out = refs[10 + 2 * SPAN :]
    rows = queries.shape[0]
    scale = HD ** (-0.5)
    factor = scale * 1.4426950408889634
    q = queries[...]
    scores = [
        dot(q, keys[i][...], ((1,), (1,))) * factor + bias[:, i * rows : (i + 1) * rows]
        for i in range(SPAN + 1)
    ]
    top = functools.reduce(jnp.maximum, scores)
    top = jnp.max(top, -1, keepdims=True)
    powers = [jnp.exp2(part - top) for part in scores]
    total = jnp.sum(functools.reduce(jnp.add, powers), -1, keepdims=True)
    inverse = 1.0 / total
    weights = [part * inverse for part in powers]
    probs = [part.astype(jnp.bfloat16) for part in weights]
    out = functools.reduce(
        jnp.add, [dot(probs[i], values[i][...], ((1,), (0,))) for i in range(SPAN + 1)]
    )
    out = out.astype(jnp.bfloat16).astype(jnp.float32)
    branch = key_branch[...].astype(jnp.float32)
    grad = mixed_grad[...]
    mixed_out[...] = (branch * out).astype(jnp.bfloat16)
    branch_out[...] = (grad * out).astype(jnp.bfloat16)
    attn_grad = (grad * branch).astype(jnp.bfloat16)
    row_dot = jnp.sum(attn_grad.astype(jnp.float32) * out, -1, keepdims=True)
    query_sum = None
    for i in range(SPAN + 1):
        prob_grad = dot(attn_grad, values[i][...], ((1,), (1,)))
        score_grad = (weights[i] * (prob_grad - row_dot)).astype(jnp.bfloat16)
        part = dot(score_grad, keys[i][...], ((1,), (0,)))
        query_sum = part if query_sum is None else query_sum + part
        target = own_out if i == SPAN else earlier_out[i]
        target[:, :HD] = (dot(score_grad, q, ((0,), (0,))) * scale).astype(target.dtype)
        target[:, HD:] = dot(probs[i], attn_grad, ((0,), (0,))).astype(target.dtype)
    query_out[...] = (query_sum * scale).astype(jnp.bfloat16)


def attention(bias, queries, key_branch, mixed_grad, keys_in, values_in, windows, chunk, heads):
    rows = queries.shape[0]
    width = heads * HD
    whole = pl.BlockSpec((rows, HD), lambda h: (0, chunk * heads + h))
    first = pl.BlockSpec((rows, HD), lambda h: (0, h))
    second = pl.BlockSpec((rows, HD), lambda h: (0, heads + h))
    pair = pl.BlockSpec((rows, 2 * HD), lambda h: (0, h))
    half = jax.ShapeDtypeStruct((rows, width), jnp.bfloat16)
    window = (SPAN + 1) * rows
    return pl.pallas_call(
        attention_kernel,
        grid=(heads,),
        in_specs=[pl.BlockSpec((rows, window), lambda h: (0, 0)), whole, whole, whole]
        + [first] * SPAN
        + [whole]
        + [second] * SPAN
        + [whole],
        out_specs=[first, first, first] + [pair] * (SPAN + 1),
        out_shape=[half, half, half, jax.ShapeDtypeStruct((rows, 2 * width), jnp.float32)]
        + [jax.ShapeDtypeStruct((rows, 2 * width), jnp.bfloat16)] * SPAN,
        compiler_params=pltpu.CompilerParams(vmem_limit_bytes=VMEM),
        cost_estimate=pl.CostEstimate(
            flops=heads * 24 * rows * window * HD,
            bytes_accessed=rows * width * 60,
            transcendentals=heads * rows * window,
        ),
    )(bias, queries, key_branch, mixed_grad, *windows, keys_in, *windows, values_in)


def last_sum_kernel(own, far, near, odd, key_out, value_out):
    partner = jnp.where(odd[...] == 0, near[...].astype(jnp.float32), 0.0)
    total = own[...] + far[...].astype(jnp.float32) + partner
    key_out[...] = total[:, :HD].astype(jnp.bfloat16)
    value_out[...] = total[:, HD:].astype(jnp.bfloat16)


def last_sum(own, far, near, odd):
    rows, width = own.shape[0], own.shape[1] // 2
    pair = pl.BlockSpec((rows, 2 * HD), lambda h: (0, h))
    single = pl.BlockSpec((rows, HD), lambda h: (0, h))
    flag = jnp.broadcast_to(odd, (1, 2 * HD)).astype(jnp.int32)
    return pl.pallas_call(
        last_sum_kernel,
        grid=(width // HD,),
        in_specs=[pair, pair, pair, pl.BlockSpec((1, 2 * HD), lambda h: (0, 0))],
        out_specs=[single, single],
        out_shape=[jax.ShapeDtypeStruct((rows, width), jnp.bfloat16)] * 2,
    )(own, far, near, flag)


def per_device(
    queries_in, keys_in, values_in, gate_branch, key_branch, mr_filter, out_grad, doc_ids
):
    shard_len = queries_in.shape[0]
    width = queries_in.shape[1]
    heads_dev = width // HD
    heads = heads_dev // CHUNKS
    span_cols = heads * HD
    window = (SPAN + 1) * shard_len
    position = lax.axis_index("seq")
    odd = position % 2
    f32 = jnp.float32

    windows = []
    for chunk in range(CHUNKS):
        cols = slice(chunk * span_cols, (chunk + 1) * span_cols)
        own = jnp.concatenate([keys_in[:, cols], values_in[:, cols]], 1)
        two = from_behind(own, "seq", 2)
        one = exchange(jnp.where(odd == 1, two, own))
        four = from_behind(two, "seq", 2)
        three = exchange(jnp.where(odd == 1, four, two))
        windows.append([four, three, two, one])

    doc_front = jnp.concatenate([jnp.full((SPAN * shard_len,), -1, jnp.int32), doc_ids], 0)
    key_doc = lax.dynamic_slice_in_dim(doc_front, position * shard_len, window, 0)
    query_doc = lax.dynamic_slice_in_dim(doc_ids, position * shard_len, shard_len, 0)
    query_pos = jnp.arange(shard_len, dtype=jnp.int32)
    key_pos = jnp.arange(window, dtype=jnp.int32) - SPAN * shard_len
    allowed = (query_doc[:, None] == key_doc[None, :]) & (key_pos[None, :] <= query_pos[:, None])
    bias = jnp.where(allowed, 0.0, -jnp.inf).astype(f32)

    conv_grad = (out_grad.astype(f32) * gate_branch.astype(f32)).astype(jnp.bfloat16)
    grad_edge = from_behind(conv_grad[: TAPS - 1], "seq", -1)
    mixed_grad = anti_conv(jnp.concatenate([conv_grad, grad_edge], 0), mr_filter)
    taps = jnp.arange(TAPS, dtype=jnp.int32)
    mirror = (taps[:, None] + taps[None, :] == TAPS - 1).astype(jnp.bfloat16)
    flipped = jnp.dot(mirror, mr_filter, preferred_element_type=jnp.bfloat16)

    mixed_parts, branch_parts, query_parts, key_parts, value_parts = [], [], [], [], []
    for chunk in range(CHUNKS):
        mixed_c, branch_c, query_c, own_t, t4, t3, t2, t1 = attention(
            bias, queries_in, key_branch, mixed_grad, keys_in, values_in, windows[chunk], chunk, heads
        )
        mixed_parts.append(mixed_c)
        branch_parts.append(branch_c)
        query_parts.append(query_c)
        e3 = exchange(t3)
        e1 = exchange(t1)
        s4 = (t4.astype(f32) + jnp.where(odd == 1, e3.astype(f32), 0.0)).astype(jnp.bfloat16)
        g4 = from_behind(s4, "seq", -2)
        s2 = (
            t2.astype(f32) + g4.astype(f32) + jnp.where(odd == 1, e1, e3).astype(f32)
        ).astype(jnp.bfloat16)
        g2 = from_behind(s2, "seq", -2)
        key_c, value_c = last_sum(own_t, g2, e1, odd)
        key_parts.append(key_c)
        value_parts.append(value_c)

    mixed = jnp.concatenate(mixed_parts, 1)
    mixed_edge = from_behind(mixed[shard_len - (TAPS - 1) :], "seq", 1)
    mixed_ext = jnp.concatenate([mixed_edge, mixed], 0)
    filter_part = filter_corr(mixed_ext, conv_grad)
    size = lax.axis_size("seq")
    tap_rows = TAPS // size
    blocks = jnp.concatenate(
        [filter_part[(size - 1 - j) * tap_rows : (size - j) * tap_rows][None] for j in range(size)], 0
    )
    received = lax.all_to_all(blocks, "seq", 0, 0)
    own_grad = jnp.flip(jnp.sum(received, 0), 0)
    conv_out = causal_conv(mixed_ext, flipped)
    gate_grad = (out_grad.astype(f32) * conv_out).astype(jnp.bfloat16)
    own_taps = lax.dynamic_slice_in_dim(mr_filter, position * tap_rows, tap_rows, 0).astype(f32)
    norms = lax.psum((jnp.sum(own_taps * own_taps), jnp.sum(own_grad * own_grad)), ("seq", "ch"))
    trust = jnp.sqrt(norms[0]) / jnp.sqrt(norms[1] + 1e-06)
    return (
        jnp.concatenate(query_parts, 1),
        jnp.concatenate(key_parts, 1),
        jnp.concatenate(value_parts, 1),
        gate_grad,
        jnp.concatenate(branch_parts, 1),
        trust * own_grad,
    )


def solution(mesh):
    return jax.shard_map(
        per_device,
        mesh=mesh,
        in_specs=(
            P("seq", "ch"),
            P("seq", "ch"),
            P("seq", "ch"),
            P("seq", "ch"),
            P("seq", "ch"),
            P(None, "ch"),
            P("seq", "ch"),
            P(),
        ),
        out_specs=(
            P("seq", "ch"),
            P("seq", "ch"),
            P("seq", "ch"),
            P("seq", "ch"),
            P("seq", "ch"),
            P("seq", "ch"),
        ),
        check_vma=False,
    )
```

```python
import functools
import jax
import jax.numpy as jnp
from jax import lax
from jax.experimental import pallas as pl
from jax.experimental.pallas import tpu as pltpu
from jax.sharding import PartitionSpec as P

HD = 128
TAPS = 128
SPAN = 4
CHUNKS = 2
LAST_HEADS = 4
VMEM = 40 * 1024 * 1024


def from_behind(array, axis, by):
    size = lax.axis_size(axis)
    pairs = [(i, i + by) for i in range(size) if 0 <= i + by < size]
    return lax.ppermute(array, axis, pairs)


def causal_conv(extended, weights_in):
    channels = extended.shape[1]
    kernel = weights_in[:, None, :]
    result = lax.conv_general_dilated(
        extended[None],
        kernel,
        (1,),
        "VALID",
        dimension_numbers=("NWC", "WIO", "NWC"),
        feature_group_count=channels,
        preferred_element_type=jnp.float32,
    )
    return result[0]


def anti_conv(extended, weights_in):
    channels = extended.shape[1]
    kernel = weights_in[:, None, :]
    result = lax.conv_general_dilated(
        extended[None],
        kernel,
        (1,),
        "VALID",
        dimension_numbers=("NWC", "WIO", "NWC"),
        feature_group_count=channels,
        preferred_element_type=jnp.float32,
    )
    return result[0]


def filter_corr(extended, gradient):
    channels = extended.shape[1]
    kernel = gradient[:, None, :]
    result = lax.conv_general_dilated(
        extended[None],
        kernel,
        (1,),
        "VALID",
        dimension_numbers=("NWC", "WIO", "NWC"),
        feature_group_count=channels,
        preferred_element_type=jnp.float32,
    )
    return result[0]


def exchange(array):
    size = lax.axis_size("seq")
    return lax.ppermute(array, "seq", [(i, i ^ 1) for i in range(size)])


def dot(a, b, dims):
    return lax.dot_general(a, b, (dims, ((), ())), preferred_element_type=jnp.float32)


def attention_kernel(*refs):
    bias, queries, key_branch, mixed_grad = refs[:4]
    keys, values = refs[4 : 5 + SPAN], refs[5 + SPAN : 6 + 2 * SPAN]
    mixed_out, branch_out, query_out, own_out = refs[6 + 2 * SPAN : 10 + 2 * SPAN]
    earlier_out = refs[10 + 2 * SPAN :]
    rows = queries.shape[0]
    scale = HD ** (-0.5)
    factor = scale * 1.4426950408889634
    q = queries[...]
    scores = [
        dot(q, keys[i][...], ((1,), (1,))) * factor + bias[:, i * rows : (i + 1) * rows]
        for i in range(SPAN + 1)
    ]
    top = functools.reduce(jnp.maximum, scores)
    top = jnp.max(top, -1, keepdims=True)
    powers = [jnp.exp2(part - top) for part in scores]
    total = jnp.sum(functools.reduce(jnp.add, powers), -1, keepdims=True)
    inverse = 1.0 / total
    weights = [part * inverse for part in powers]
    probs = [part.astype(jnp.bfloat16) for part in weights]
    out = functools.reduce(
        jnp.add, [dot(probs[i], values[i][...], ((1,), (0,))) for i in range(SPAN + 1)]
    )
    out = out.astype(jnp.bfloat16).astype(jnp.float32)
    branch = key_branch[...].astype(jnp.float32)
    grad = mixed_grad[...]
    mixed_out[...] = (branch * out).astype(jnp.bfloat16)
    branch_out[...] = (grad * out).astype(jnp.bfloat16)
    attn_grad = (grad * branch).astype(jnp.bfloat16)
    row_dot = jnp.sum(attn_grad.astype(jnp.float32) * out, -1, keepdims=True)
    query_sum = None
    for i in range(SPAN + 1):
        prob_grad = dot(attn_grad, values[i][...], ((1,), (1,)))
        score_grad = (weights[i] * (prob_grad - row_dot)).astype(jnp.bfloat16)
        part = dot(score_grad, keys[i][...], ((1,), (0,)))
        query_sum = part if query_sum is None else query_sum + part
        target = own_out if i == SPAN else earlier_out[i]
        target[:, :HD] = (dot(score_grad, q, ((0,), (0,))) * scale).astype(target.dtype)
        target[:, HD:] = dot(probs[i], attn_grad, ((0,), (0,))).astype(target.dtype)
    query_out[...] = (query_sum * scale).astype(jnp.bfloat16)


def attention(bias, queries, key_branch, mixed_grad, keys_in, values_in, windows, chunk, heads):
    rows = queries.shape[0]
    width = heads * HD
    whole = pl.BlockSpec((rows, HD), lambda h: (0, chunk * heads + h))
    first = pl.BlockSpec((rows, HD), lambda h: (0, h))
    second = pl.BlockSpec((rows, HD), lambda h: (0, heads + h))
    pair = pl.BlockSpec((rows, 2 * HD), lambda h: (0, h))
    half = jax.ShapeDtypeStruct((rows, width), jnp.bfloat16)
    window = (SPAN + 1) * rows
    return pl.pallas_call(
        attention_kernel,
        grid=(heads,),
        in_specs=[pl.BlockSpec((rows, window), lambda h: (0, 0)), whole, whole, whole]
        + [first] * SPAN
        + [whole]
        + [second] * SPAN
        + [whole],
        out_specs=[first, first, first] + [pair] * (SPAN + 1),
        out_shape=[half, half, half, jax.ShapeDtypeStruct((rows, 2 * width), jnp.float32)]
        + [jax.ShapeDtypeStruct((rows, 2 * width), jnp.bfloat16)] * SPAN,
        compiler_params=pltpu.CompilerParams(vmem_limit_bytes=VMEM),
        cost_estimate=pl.CostEstimate(
            flops=heads * 24 * rows * window * HD,
            bytes_accessed=rows * width * 60,
            transcendentals=heads * rows * window,
        ),
    )(bias, queries, key_branch, mixed_grad, *windows, keys_in, *windows, values_in)


def last_sum_kernel(own, far, near, odd, key_out, value_out):
    for head in range(LAST_HEADS):
        wide = slice(head * 2 * HD, (head + 1) * 2 * HD)
        narrow = slice(head * HD, (head + 1) * HD)
        partner = jnp.where(odd[...] == 0, near[:, wide].astype(jnp.float32), 0.0)
        total = own[:, wide] + far[:, wide].astype(jnp.float32) + partner
        key_out[:, narrow] = total[:, :HD].astype(jnp.bfloat16)
        value_out[:, narrow] = total[:, HD:].astype(jnp.bfloat16)


def last_sum(own, far, near, odd):
    rows, width = own.shape[0], own.shape[1] // 2
    pair = pl.BlockSpec((rows, LAST_HEADS * 2 * HD), lambda h: (0, h))
    single = pl.BlockSpec((rows, LAST_HEADS * HD), lambda h: (0, h))
    flag = jnp.broadcast_to(odd, (1, 2 * HD)).astype(jnp.int32)
    return pl.pallas_call(
        last_sum_kernel,
        grid=(width // (LAST_HEADS * HD),),
        in_specs=[pair, pair, pair, pl.BlockSpec((1, 2 * HD), lambda h: (0, 0))],
        out_specs=[single, single],
        out_shape=[jax.ShapeDtypeStruct((rows, width), jnp.bfloat16)] * 2,
    )(own, far, near, flag)


def per_device(
    queries_in, keys_in, values_in, gate_branch, key_branch, mr_filter, out_grad, doc_ids
):
    shard_len = queries_in.shape[0]
    width = queries_in.shape[1]
    heads_dev = width // HD
    heads = heads_dev // CHUNKS
    span_cols = heads * HD
    window = (SPAN + 1) * shard_len
    position = lax.axis_index("seq")
    odd = position % 2
    f32 = jnp.float32

    columns = [slice(c * span_cols, (c + 1) * span_cols) for c in range(CHUNKS)]
    owns = [jnp.concatenate([keys_in[:, c], values_in[:, c]], 1) for c in columns]
    twos = [from_behind(own, "seq", 2) for own in owns]

    doc_front = jnp.concatenate([jnp.full((SPAN * shard_len,), -1, jnp.int32), doc_ids], 0)
    key_doc = lax.dynamic_slice_in_dim(doc_front, position * shard_len, window, 0)
    query_doc = lax.dynamic_slice_in_dim(doc_ids, position * shard_len, shard_len, 0)
    query_pos = jnp.arange(shard_len, dtype=jnp.int32)
    key_pos = jnp.arange(window, dtype=jnp.int32) - SPAN * shard_len
    allowed = (query_doc[:, None] == key_doc[None, :]) & (key_pos[None, :] <= query_pos[:, None])
    bias = jnp.where(allowed, 0.0, -jnp.inf).astype(f32)

    conv_grad = (out_grad.astype(f32) * gate_branch.astype(f32)).astype(jnp.bfloat16)
    grad_edge = from_behind(conv_grad[: TAPS - 1], "seq", -1)
    mixed_grad = anti_conv(jnp.concatenate([conv_grad, grad_edge], 0), mr_filter)
    taps = jnp.arange(TAPS, dtype=jnp.int32)
    mirror = (taps[:, None] + taps[None, :] == TAPS - 1).astype(jnp.bfloat16)
    flipped = jnp.dot(mirror, mr_filter, preferred_element_type=jnp.bfloat16)

    mixed_grad, bias, flipped, *twos = lax.optimization_barrier((mixed_grad, bias, flipped, *twos))
    ones = [exchange(jnp.where(odd == 1, two, own)) for own, two in zip(owns, twos)]
    fours = [from_behind(two, "seq", 2) for two in twos]
    ones, fours = lax.optimization_barrier((ones, fours))
    threes = [exchange(jnp.where(odd == 1, four, two)) for four, two in zip(fours, twos)]
    windows = [list(window) for window in zip(fours, threes, twos, ones)]

    size = lax.axis_size("seq")
    tap_rows = TAPS // size
    query_parts, branch_parts, gate_parts, filter_parts, sums = [], [], [], [], []
    sources = (queries_in, key_branch, mixed_grad, keys_in, values_in, *windows[0])
    for chunk in range(CHUNKS):
        cols = columns[chunk]
        mixed, branch_c, query_c, own_t, t4, t3, t2, t1 = attention(
            bias, *sources[:5], sources[5:], chunk, heads
        )
        branch_parts.append(branch_c)
        query_parts.append(query_c)
        e3 = exchange(t3)
        e1 = exchange(t1)
        mixed_edge = from_behind(mixed[shard_len - (TAPS - 1) :], "seq", 1)
        mixed_ext = jnp.concatenate([mixed_edge, mixed], 0)
        filter_part = filter_corr(mixed_ext, conv_grad[:, cols])
        conv_out = causal_conv(mixed_ext, flipped[:, cols])
        gate_c = (out_grad[:, cols].astype(f32) * conv_out).astype(jnp.bfloat16)
        if chunk + 1 < CHUNKS:
            gate_c, filter_part, e3, *rest = lax.optimization_barrier(
                (gate_c, filter_part, e3, *sources[:5], *windows[chunk + 1])
            )
            sources = tuple(rest)
        gate_parts.append(gate_c)
        blocks = jnp.concatenate(
            [
                filter_part[(size - 1 - j) * tap_rows : (size - j) * tap_rows][None]
                for j in range(size)
            ],
            0,
        )
        received = lax.all_to_all(blocks, "seq", 0, 0)
        filter_parts.append(jnp.sum(received, 0))
        s4 = (t4.astype(f32) + jnp.where(odd == 1, e3.astype(f32), 0.0)).astype(jnp.bfloat16)
        g4 = from_behind(s4, "seq", -2)
        s2 = (
            t2.astype(f32) + g4.astype(f32) + jnp.where(odd == 1, e1, e3).astype(f32)
        ).astype(jnp.bfloat16)
        g2 = from_behind(s2, "seq", -2)
        sums.append((own_t, g2, e1))

    own_grad = jnp.flip(jnp.concatenate(filter_parts, 1), 0)
    own_taps = lax.dynamic_slice_in_dim(mr_filter, position * tap_rows, tap_rows, 0).astype(f32)
    norms = lax.psum((jnp.sum(own_taps * own_taps), jnp.sum(own_grad * own_grad)), ("seq", "ch"))
    trust = jnp.sqrt(norms[0]) / jnp.sqrt(norms[1] + 1e-06)
    ends = [last_sum(*terms, odd) for terms in sums]
    return (
        jnp.concatenate(query_parts, 1),
        jnp.concatenate([end[0] for end in ends], 1),
        jnp.concatenate([end[1] for end in ends], 1),
        jnp.concatenate(gate_parts, 1),
        jnp.concatenate(branch_parts, 1),
        trust * own_grad,
    )


def solution(mesh):
    return jax.shard_map(
        per_device,
        mesh=mesh,
        in_specs=(
            P("seq", "ch"),
            P("seq", "ch"),
            P("seq", "ch"),
            P("seq", "ch"),
            P("seq", "ch"),
            P(None, "ch"),
            P("seq", "ch"),
            P(),
        ),
        out_specs=(
            P("seq", "ch"),
            P("seq", "ch"),
            P("seq", "ch"),
            P("seq", "ch"),
            P("seq", "ch"),
            P("seq", "ch"),
        ),
        check_vma=False,
    )
```

```python
import functools
import jax
import jax.numpy as jnp
from jax import lax
from jax.experimental import pallas as pl
from jax.experimental.pallas import tpu as pltpu
from jax.sharding import PartitionSpec as P

HD = 128
TAPS = 128
SPAN = 4
CHUNKS = 2
LAST_HEADS = 4
VMEM = 40 * 1024 * 1024


def from_behind(array, axis, by):
    size = lax.axis_size(axis)
    pairs = [(i, i + by) for i in range(size) if 0 <= i + by < size]
    return lax.ppermute(array, axis, pairs)


def causal_conv(extended, weights_in):
    channels = extended.shape[1]
    kernel = weights_in[:, None, :]
    result = lax.conv_general_dilated(
        extended[None],
        kernel,
        (1,),
        "VALID",
        dimension_numbers=("NWC", "WIO", "NWC"),
        feature_group_count=channels,
        preferred_element_type=jnp.float32,
    )
    return result[0]


def anti_conv(extended, weights_in):
    channels = extended.shape[1]
    kernel = weights_in[:, None, :]
    result = lax.conv_general_dilated(
        extended[None],
        kernel,
        (1,),
        "VALID",
        dimension_numbers=("NWC", "WIO", "NWC"),
        feature_group_count=channels,
        preferred_element_type=jnp.float32,
    )
    return result[0]


def filter_corr(extended, gradient):
    channels = extended.shape[1]
    kernel = gradient[:, None, :]
    result = lax.conv_general_dilated(
        extended[None],
        kernel,
        (1,),
        "VALID",
        dimension_numbers=("NWC", "WIO", "NWC"),
        feature_group_count=channels,
        preferred_element_type=jnp.float32,
    )
    return result[0]


def exchange(array):
    size = lax.axis_size("seq")
    return lax.ppermute(array, "seq", [(i, i ^ 1) for i in range(size)])


def dot(a, b, dims):
    return lax.dot_general(a, b, (dims, ((), ())), preferred_element_type=jnp.float32)


def attention_kernel(*refs):
    bias, queries, key_branch, mixed_grad = refs[:4]
    keys, values = refs[4 : 5 + SPAN], refs[5 + SPAN : 6 + 2 * SPAN]
    mixed_out, branch_out, query_out, own_out = refs[6 + 2 * SPAN : 10 + 2 * SPAN]
    earlier_out = refs[10 + 2 * SPAN :]
    rows = queries.shape[0]
    scale = HD ** (-0.5)
    factor = scale * 1.4426950408889634
    q = queries[...]
    scores = [
        dot(q, keys[i][...], ((1,), (1,))) * factor + bias[:, i * rows : (i + 1) * rows]
        for i in range(SPAN + 1)
    ]
    top = functools.reduce(jnp.maximum, scores)
    top = jnp.max(top, -1, keepdims=True)
    powers = [jnp.exp2(part - top) for part in scores]
    total = jnp.sum(functools.reduce(jnp.add, powers), -1, keepdims=True)
    inverse = 1.0 / total
    weights = [part * inverse for part in powers]
    probs = [part.astype(jnp.bfloat16) for part in weights]
    out = functools.reduce(
        jnp.add, [dot(probs[i], values[i][...], ((1,), (0,))) for i in range(SPAN + 1)]
    )
    out = out.astype(jnp.bfloat16).astype(jnp.float32)
    branch = key_branch[...].astype(jnp.float32)
    grad = mixed_grad[...]
    mixed_out[...] = (branch * out).astype(jnp.bfloat16)
    branch_out[...] = (grad * out).astype(jnp.bfloat16)
    attn_grad = (grad * branch).astype(jnp.bfloat16)
    row_dot = jnp.sum(attn_grad.astype(jnp.float32) * out, -1, keepdims=True)
    query_sum = None
    for i in range(SPAN + 1):
        prob_grad = dot(attn_grad, values[i][...], ((1,), (1,)))
        score_grad = (weights[i] * (prob_grad - row_dot)).astype(jnp.bfloat16)
        part = dot(score_grad, keys[i][...], ((1,), (0,)))
        query_sum = part if query_sum is None else query_sum + part
        target = own_out if i == SPAN else earlier_out[i]
        target[:, :HD] = (dot(score_grad, q, ((0,), (0,))) * scale).astype(target.dtype)
        target[:, HD:] = dot(probs[i], attn_grad, ((0,), (0,))).astype(target.dtype)
    query_out[...] = (query_sum * scale).astype(jnp.bfloat16)


def attention(bias, queries, key_branch, mixed_grad, keys_in, values_in, windows, chunk, heads):
    rows = queries.shape[0]
    width = heads * HD
    whole = pl.BlockSpec((rows, HD), lambda h: (0, chunk * heads + h))
    first = pl.BlockSpec((rows, HD), lambda h: (0, h))
    second = pl.BlockSpec((rows, HD), lambda h: (0, heads + h))
    pair = pl.BlockSpec((rows, 2 * HD), lambda h: (0, h))
    half = jax.ShapeDtypeStruct((rows, width), jnp.bfloat16)
    window = (SPAN + 1) * rows
    return pl.pallas_call(
        attention_kernel,
        grid=(heads,),
        in_specs=[pl.BlockSpec((rows, window), lambda h: (0, 0)), whole, whole, first]
        + [first] * SPAN
        + [whole]
        + [second] * SPAN
        + [whole],
        out_specs=[first, first, first] + [pair] * (SPAN + 1),
        out_shape=[half, half, half, jax.ShapeDtypeStruct((rows, 2 * width), jnp.float32)]
        + [jax.ShapeDtypeStruct((rows, 2 * width), jnp.bfloat16)] * SPAN,
        compiler_params=pltpu.CompilerParams(vmem_limit_bytes=VMEM),
        cost_estimate=pl.CostEstimate(
            flops=heads * 24 * rows * window * HD,
            bytes_accessed=rows * width * 60,
            transcendentals=heads * rows * window,
        ),
    )(bias, queries, key_branch, mixed_grad, *windows, keys_in, *windows, values_in)


def last_sum_kernel(own, far, near, odd, key_out, value_out):
    for head in range(LAST_HEADS):
        wide = slice(head * 2 * HD, (head + 1) * 2 * HD)
        narrow = slice(head * HD, (head + 1) * HD)
        partner = jnp.where(odd[...] == 0, near[:, wide].astype(jnp.float32), 0.0)
        total = own[:, wide] + far[:, wide].astype(jnp.float32) + partner
        key_out[:, narrow] = total[:, :HD].astype(jnp.bfloat16)
        value_out[:, narrow] = total[:, HD:].astype(jnp.bfloat16)


def last_sum(own, far, near, odd):
    rows, width = own.shape[0], own.shape[1] // 2
    pair = pl.BlockSpec((rows, LAST_HEADS * 2 * HD), lambda h: (0, h))
    single = pl.BlockSpec((rows, LAST_HEADS * HD), lambda h: (0, h))
    flag = jnp.broadcast_to(odd, (1, 2 * HD)).astype(jnp.int32)
    return pl.pallas_call(
        last_sum_kernel,
        grid=(width // (LAST_HEADS * HD),),
        in_specs=[pair, pair, pair, pl.BlockSpec((1, 2 * HD), lambda h: (0, 0))],
        out_specs=[single, single],
        out_shape=[jax.ShapeDtypeStruct((rows, width), jnp.bfloat16)] * 2,
    )(own, far, near, flag)


def per_device(
    queries_in, keys_in, values_in, gate_branch, key_branch, mr_filter, out_grad, doc_ids
):
    shard_len = queries_in.shape[0]
    width = queries_in.shape[1]
    heads_dev = width // HD
    heads = heads_dev // CHUNKS
    span_cols = heads * HD
    window = (SPAN + 1) * shard_len
    position = lax.axis_index("seq")
    odd = position % 2
    f32 = jnp.float32

    columns = [slice(c * span_cols, (c + 1) * span_cols) for c in range(CHUNKS)]
    owns = [jnp.concatenate([keys_in[:, c], values_in[:, c]], 1) for c in columns]
    twos = [from_behind(own, "seq", 2) for own in owns]

    doc_front = jnp.concatenate([jnp.full((SPAN * shard_len,), -1, jnp.int32), doc_ids], 0)
    key_doc = lax.dynamic_slice_in_dim(doc_front, position * shard_len, window, 0)
    query_doc = lax.dynamic_slice_in_dim(doc_ids, position * shard_len, shard_len, 0)
    query_pos = jnp.arange(shard_len, dtype=jnp.int32)
    key_pos = jnp.arange(window, dtype=jnp.int32) - SPAN * shard_len
    allowed = (query_doc[:, None] == key_doc[None, :]) & (key_pos[None, :] <= query_pos[:, None])
    bias = jnp.where(allowed, 0.0, -jnp.inf).astype(f32)

    conv_grad = (out_grad.astype(f32) * gate_branch.astype(f32)).astype(jnp.bfloat16)
    grad_edge = from_behind(conv_grad[: TAPS - 1], "seq", -1)
    grad_ext = jnp.concatenate([conv_grad, grad_edge], 0)
    taps = jnp.arange(TAPS, dtype=jnp.int32)
    mirror = (taps[:, None] + taps[None, :] == TAPS - 1).astype(jnp.bfloat16)
    flipped = jnp.dot(mirror, mr_filter, preferred_element_type=jnp.bfloat16)

    bias, flipped, grad_ext = lax.optimization_barrier((bias, flipped, grad_ext))
    mixed_grads, ones, fours = [], [], []
    for c, own, two in zip(columns, owns, twos):
        grad_c = anti_conv(grad_ext[:, c], mr_filter[:, c])
        grad_c, two, grad_ext = lax.optimization_barrier((grad_c, two, grad_ext))
        mixed_grads.append(grad_c)
        ones.append(exchange(jnp.where(odd == 1, two, own)))
        fours.append(from_behind(two, "seq", 2))
    ones[0], fours[0] = lax.optimization_barrier((ones[0], fours[0]))
    threes = [exchange(jnp.where(odd == 1, four, two)) for four, two in zip(fours, twos)]
    windows = [list(window) for window in zip(fours, threes, twos, ones)]

    size = lax.axis_size("seq")
    tap_rows = TAPS // size
    query_parts, branch_parts, gate_parts, filter_parts, sums = [], [], [], [], []
    sources = (queries_in, key_branch, mixed_grads[0], keys_in, values_in, *windows[0])
    for chunk in range(CHUNKS):
        cols = columns[chunk]
        mixed, branch_c, query_c, own_t, t4, t3, t2, t1 = attention(
            bias, *sources[:5], sources[5:], chunk, heads
        )
        branch_parts.append(branch_c)
        query_parts.append(query_c)
        e3 = exchange(t3)
        e1 = exchange(t1)
        mixed_edge = from_behind(mixed[shard_len - (TAPS - 1) :], "seq", 1)
        mixed_ext = jnp.concatenate([mixed_edge, mixed], 0)
        filter_part = filter_corr(mixed_ext, conv_grad[:, cols])
        conv_out = causal_conv(mixed_ext, flipped[:, cols])
        gate_c = (out_grad[:, cols].astype(f32) * conv_out).astype(jnp.bfloat16)
        if chunk + 1 < CHUNKS:
            gate_c, filter_part, e3, *rest = lax.optimization_barrier(
                (
                    gate_c,
                    filter_part,
                    e3,
                    *sources[:2],
                    mixed_grads[chunk + 1],
                    *sources[3:5],
                    *windows[chunk + 1],
                )
            )
            sources = tuple(rest)
        gate_parts.append(gate_c)
        blocks = jnp.concatenate(
            [
                filter_part[(size - 1 - j) * tap_rows : (size - j) * tap_rows][None]
                for j in range(size)
            ],
            0,
        )
        received = lax.all_to_all(blocks, "seq", 0, 0)
        filter_parts.append(jnp.sum(received, 0))
        s4 = (t4.astype(f32) + jnp.where(odd == 1, e3.astype(f32), 0.0)).astype(jnp.bfloat16)
        g4 = from_behind(s4, "seq", -2)
        s2 = (
            t2.astype(f32) + g4.astype(f32) + jnp.where(odd == 1, e1, e3).astype(f32)
        ).astype(jnp.bfloat16)
        g2 = from_behind(s2, "seq", -2)
        sums.append((own_t, g2, e1))

    own_grad = jnp.flip(jnp.concatenate(filter_parts, 1), 0)
    own_taps = lax.dynamic_slice_in_dim(mr_filter, position * tap_rows, tap_rows, 0).astype(f32)
    norms = jnp.stack([jnp.sum(own_taps * own_taps), jnp.sum(own_grad * own_grad)])
    norms = lax.psum(lax.psum(norms, "ch"), "seq")
    trust = jnp.sqrt(norms[0]) / jnp.sqrt(norms[1] + 1e-06)
    ends = [last_sum(*terms, odd) for terms in sums]
    return (
        jnp.concatenate(query_parts, 1),
        jnp.concatenate([end[0] for end in ends], 1),
        jnp.concatenate([end[1] for end in ends], 1),
        jnp.concatenate(gate_parts, 1),
        jnp.concatenate(branch_parts, 1),
        trust * own_grad,
    )


def solution(mesh):
    return jax.shard_map(
        per_device,
        mesh=mesh,
        in_specs=(
            P("seq", "ch"),
            P("seq", "ch"),
            P("seq", "ch"),
            P("seq", "ch"),
            P("seq", "ch"),
            P(None, "ch"),
            P("seq", "ch"),
            P(),
        ),
        out_specs=(
            P("seq", "ch"),
            P("seq", "ch"),
            P("seq", "ch"),
            P("seq", "ch"),
            P("seq", "ch"),
            P("seq", "ch"),
        ),
        check_vma=False,
    )
```
